32 devices in a mesh: grp: 4 (over z), dp: 8 (over y, x, core).
Axes of the slice: x: 2, y: 2, z: 4, core: 2. Of those that a mesh axis runs over, the one named last changes fastest.
Arguments:
- audio: bfloat16 [32, 15360], P(('grp', 'dp')), may hold values from -6 to 6
- starts: int32 [96], P(('grp', 'dp')), may hold values from 0 to 12800
- offsets: int32 [32, 2, 32], P(('grp', 'dp')), may hold values from 0 to 383
- w_first: bfloat16 [10, 512], replicated, may hold values from -2 to 2
- w_second: bfloat16 [4096, 512], replicated, may hold values from -0.09375 to 0.09375
- gain: float32 [512], replicated, may hold values from 0.5 to 10, as said below
- w_context: bfloat16 [1024, 512], replicated, may hold values from -0.1875 to 0.1875
- w_predict: bfloat16 [2, 512, 512], replicated, may hold values from -0.25 to 0.25
Outputs:
- loss: float32 [], replicated
- grad_first: float32 [10, 512], replicated
- grad_second: float32 [4096, 512], P('dp')
- grad_gain: float32 [512], replicated
- grad_context: float32 [1024, 512], P('dp')
- grad_predict: float32 [2, 512, 512], P(None, 'dp')
The draws below stay inside these ranges and needn't reach their ends.
Inputs may be any that keep to these rules, and one draw needn't show every extreme that they name: `starts`: first sample of a window. `offsets`: a latent row of the recording. `gain`: positive gains.
All inputs are finite; a program needn't handle non-finite values.
Results may differ from the reference program's by a relative error of at most 0.0085.
The reference program's roundings to bfloat16 on the way count: a program that leaves them out, or rounds other values in their place, can miss the bound.
Values may be sent and summed in bfloat16 or wider, within the bound.
A program may use at most 128 MiB of HBM per device.

```python
import math
import jax
import jax.numpy as jnp
from jax import lax

D = 512
HORIZONS = 2
STEPS = 128
NEG_DEV = 32
WIN_DEV = 3
TOK_DEV = 384
WIN_LEN = 2560
REC_LEN = 15360
RECORDS = 32
WINDOWS = 96
N_GRP = 4
N_DP = 8


def draw_gain(key, part):
    return jax.random.uniform(key, (D,), jnp.float32, 0.5, 2.0)


def with_ends(entries, rng, low, largest):
    index_at = [jax.random.randint(jax.random.fold_in(rng, axis), (), 0, length) for axis, length in enumerate(entries.shape)]
    widest = entries.shape.index(max(entries.shape))
    neighbour = index_at[:widest] + [(index_at[widest] + 1) % entries.shape[widest]] + index_at[widest + 1:]
    return entries.at[tuple(index_at)].set(low).at[tuple(neighbour)].set(largest)


def block_levels(stream_key, dims, pieces, low, largest):
    level = 1.0
    for axis_at, shards_of in pieces:
        heights = jax.random.uniform(jax.random.fold_in(jax.random.fold_in(stream_key, 6), axis_at), (shards_of,), jnp.float32, low / len(pieces), largest / len(pieces))
        level = level * jnp.repeat(jnp.exp(heights), dims[axis_at] // shards_of).reshape((-1,) + (1,) * (len(dims) - 1 - axis_at))
    return level


def noise(key, shape, scale, limit, cuts=(), kind=jnp.bfloat16):
    drawn = jax.random.normal(key, shape, jnp.float32) * scale
    if len(cuts) > 0:
        drawn = block_levels(key, shape, cuts, -0.22, 0.18) * drawn
    return jnp.clip(drawn, min=-limit, max=limit).astype(kind)


def setup_inputs(seed: int = 0) -> dict:
    streams_of = jax.random.split(jax.random.key(seed), 9)
    return {
        "audio": noise(streams_of[0], (RECORDS, REC_LEN), 1.0, 6.0, ((0, 32),)),
        "starts": with_ends(jax.random.randint(streams_of[1], (WINDOWS,), 0, REC_LEN - WIN_LEN + 1), jax.random.fold_in(streams_of[1], 1), 0, REC_LEN - WIN_LEN).astype(jnp.int32),
        "offsets": with_ends(jax.random.randint(streams_of[2], (RECORDS, HORIZONS, NEG_DEV), 0, TOK_DEV), jax.random.fold_in(streams_of[2], 1), 0, TOK_DEV - 1).astype(jnp.int32),
        "w_first": noise(streams_of[3], (10, D), 10 ** -0.5, 2.0),
        "w_second": noise(streams_of[4], (8 * D, D), (8 * D) ** -0.5, 0.09375),
        "gain": draw_gain(jax.random.fold_in(streams_of[8], 71), 0),
        "w_context": noise(streams_of[6], (2 * D, D), (2 * D) ** -0.5, 0.1875),
        "w_predict": noise(streams_of[7], (HORIZONS, D, D), D ** -0.5, 0.25),
    }


def shift_rows(values):
    return jnp.concatenate([jnp.zeros_like(values[:, :1]), values[:, :-1]], axis=1)

def shift_back(values):
    return jnp.concatenate([values[:, 1:], jnp.zeros_like(values[:, :1])], axis=1)

def future_rows(values, horizon):
    return jnp.concatenate([values[:, horizon:], jnp.zeros_like(values[:, :horizon])], axis=1)

def past_rows(values, horizon):
    return jnp.concatenate([jnp.zeros_like(values[:, :horizon]), values[:, :-horizon]], axis=1)

def encode(audio_row, starts_row, w_first, w_second, gain, w_context, w_predict):
    channels = w_second.shape[1]
    windows = starts_row.shape[0]
    span = 20 * STEPS
    waves = jax.vmap(lambda window_start: lax.dynamic_slice_in_dim(audio_row, window_start, span))(starts_row)
    frames = waves.reshape(windows, 4 * STEPS, 5)
    inputs_one = jnp.concatenate([shift_rows(frames), frames], axis=2).reshape(windows * 4 * STEPS, 10)
    pre_one = jnp.dot(inputs_one, w_first, preferred_element_type=jnp.float32)
    hidden_one = jax.nn.relu(pre_one).astype(jnp.bfloat16)
    grouped = hidden_one.reshape(windows, STEPS, 4 * channels)
    inputs_two = jnp.concatenate([shift_rows(grouped), grouped], axis=2).reshape(windows * STEPS, 8 * channels)
    pre_two = jnp.dot(inputs_two, w_second, preferred_element_type=jnp.float32)
    active = jax.nn.relu(pre_two)
    centred = active - lax.optimization_barrier(jnp.mean(active, axis=1, keepdims=True))
    inv_std = lax.rsqrt(lax.optimization_barrier(jnp.mean(centred * centred, axis=1, keepdims=True)) + 1e-05)
    normed = centred * inv_std
    latent = (normed * gain).astype(jnp.bfloat16)
    latent_win = latent.reshape(windows, STEPS, channels)
    context_in = jnp.concatenate([shift_rows(latent_win), latent_win], axis=2).reshape(windows * STEPS, 2 * channels)
    context = jnp.dot(context_in, w_context, preferred_element_type=jnp.float32).astype(jnp.bfloat16)
    predicted = jnp.stack([jnp.dot(context, w_predict[horizon_index], preferred_element_type=jnp.float32) for horizon_index in range(w_predict.shape[0])]).astype(jnp.bfloat16)
    return (inputs_one, pre_one, inputs_two, pre_two, normed, inv_std, latent, context_in, context, predicted)

def head(latent, predicted, panel, valid_total, scale):
    channels = latent.shape[1]
    windows = latent.shape[0] // STEPS
    latent_win = latent.reshape(windows, STEPS, channels)
    loss_sum = jnp.zeros((), jnp.float32)
    grad_latent = jnp.zeros((windows, STEPS, channels), jnp.float32)
    weight_list = []
    query_list = []
    for horizon_index in range(predicted.shape[0]):
        horizon = horizon_index + 1
        query = predicted[horizon_index]
        target = future_rows(latent_win, horizon).reshape(windows * STEPS, channels)
        valid = jnp.tile((jnp.arange(STEPS) + horizon < STEPS).astype(jnp.float32), windows)
        positive = lax.optimization_barrier(jnp.sum(query.astype(jnp.float32) * target.astype(jnp.float32), axis=1)) * scale
        panel_rows = panel[:, horizon_index, :]
        negative = jnp.dot(query, panel_rows.T, preferred_element_type=jnp.float32) * scale
        highest = jnp.maximum(positive, lax.optimization_barrier(jnp.max(negative, axis=1)))
        denominator = jnp.exp(positive - highest) + lax.optimization_barrier(jnp.sum(jnp.exp(negative - highest[:, None]), axis=1))
        log_total = highest + jnp.log(denominator)
        loss_sum = loss_sum + jnp.sum(valid * (log_total - positive))
        pos_grad = valid * (jnp.exp(positive - log_total) - 1.0) * (scale / valid_total)
        neg_weights = (valid[:, None] * jnp.exp(negative - log_total[:, None]) * (scale / valid_total)).astype(jnp.bfloat16)
        query_grad = (pos_grad[:, None] * target.astype(jnp.float32) + jnp.dot(neg_weights, panel_rows, preferred_element_type=jnp.float32)).astype(jnp.bfloat16)
        grad_latent = grad_latent + past_rows((pos_grad[:, None] * query.astype(jnp.float32)).reshape(windows, STEPS, channels), horizon)
        weight_list.append(neg_weights)
        query_list.append(query_grad)
    return (loss_sum, jnp.stack(weight_list), jnp.stack(query_list), grad_latent.reshape(windows * STEPS, channels))

def add_own(grad_latent, picks, owned):
    for horizon_index in range(picks.shape[0]):
        grad_latent = grad_latent.at[picks[horizon_index]].add(owned[:, horizon_index, :])
    return grad_latent

def backward(saved, grad_latent, query_grads, w_first, w_second, gain, w_context, w_predict):
    inputs_one, pre_one, inputs_two, pre_two, normed, inv_std, latent, context_in, context, predicted = saved
    channels = w_second.shape[1]
    windows = latent.shape[0] // STEPS
    grad_predict = jnp.stack([jnp.dot(context.T, query_grads[horizon_index], preferred_element_type=jnp.float32) for horizon_index in range(w_predict.shape[0])])
    context_sum = jnp.dot(query_grads[0], w_predict[0].T, preferred_element_type=jnp.float32)
    for horizon_index in range(1, w_predict.shape[0]):
        context_sum = context_sum + jnp.dot(query_grads[horizon_index], w_predict[horizon_index].T, preferred_element_type=jnp.float32)
    context_grad = context_sum.astype(jnp.bfloat16)
    grad_context = jnp.dot(context_in.T, context_grad, preferred_element_type=jnp.float32)
    back_in = jnp.dot(context_grad, w_context.T, preferred_element_type=jnp.float32).reshape(windows, STEPS, 2 * channels)
    latent_total = grad_latent.reshape(windows, STEPS, channels) + back_in[:, :, channels:] + shift_back(back_in[:, :, :channels])
    latent_total = latent_total.reshape(windows * STEPS, channels)
    grad_gain = lax.optimization_barrier(jnp.sum(latent_total * normed, axis=0))
    normed_grad = latent_total * gain
    active_grad = inv_std * (normed_grad - lax.optimization_barrier(jnp.mean(normed_grad, axis=1, keepdims=True)) - normed * lax.optimization_barrier(jnp.mean(normed_grad * normed, axis=1, keepdims=True)))
    pre_two_grad = jnp.where(pre_two > 0, active_grad, 0.0).astype(jnp.bfloat16)
    grad_second = jnp.dot(inputs_two.T, pre_two_grad, preferred_element_type=jnp.float32)
    back_two = jnp.dot(pre_two_grad, w_second.T, preferred_element_type=jnp.float32).reshape(windows, STEPS, 8 * channels)
    grouped_grad = back_two[:, :, 4 * channels:] + shift_back(back_two[:, :, :4 * channels])
    hidden_grad = grouped_grad.reshape(windows * 4 * STEPS, channels)
    pre_one_grad = jnp.where(pre_one > 0, hidden_grad, 0.0).astype(jnp.bfloat16)
    grad_first = jnp.dot(inputs_one.T, pre_one_grad, preferred_element_type=jnp.float32)
    return (grad_first, grad_second, grad_gain, grad_context, grad_predict)

def reference(audio, starts, offsets, w_first, w_second, gain, w_context, w_predict):
    horizons = w_predict.shape[0]
    scale = 1.0 / math.sqrt(D)
    valid_total = float(WINDOWS * (horizons * STEPS - horizons * (horizons + 1) // 2))
    starts_rec = starts.reshape(RECORDS, WIN_DEV)

    def group_part(group):
        first = (group * N_DP).astype(jnp.int32)
        audio_grp = lax.dynamic_slice_in_dim(audio, first, N_DP, 0)
        starts_grp = lax.dynamic_slice_in_dim(starts_rec, first, N_DP, 0)
        offsets_grp = lax.dynamic_slice_in_dim(offsets, first, N_DP, 0)
        saved = jax.vmap(encode, in_axes=(0, 0, None, None, None, None, None))(audio_grp, starts_grp, w_first, w_second, gain, w_context, w_predict)
        latent = saved[6]
        predicted = saved[9]
        chosen = jax.vmap(lambda rows, picks: rows[picks])(latent, offsets_grp)
        panel = chosen.transpose(0, 2, 1, 3).reshape(N_DP * NEG_DEV, horizons, D)
        loss_sum, neg_weights, query_grads, grad_latent = jax.vmap(head, in_axes=(0, 0, None, None, None))(latent, predicted, panel, valid_total, scale)
        panel_grad = jnp.einsum('aktn,aktd->nkd', neg_weights.astype(jnp.float32), predicted.astype(jnp.float32))
        owned = panel_grad.reshape(N_DP, NEG_DEV, horizons, D)
        grad_latent = jax.vmap(add_own)(grad_latent, offsets_grp, owned)
        grads = jax.vmap(backward, in_axes=(0, 0, 0, None, None, None, None, None))(saved, grad_latent, query_grads, w_first, w_second, gain, w_context, w_predict)
        return (jnp.sum(loss_sum),) + tuple((lax.optimization_barrier(jnp.sum(piece, axis=0)) for piece in grads))
    results = lax.map(group_part, jnp.arange(N_GRP, dtype=jnp.int32))
    sums = [lax.optimization_barrier(jnp.sum(piece, axis=0)) for piece in results]
    return (sums[0] / valid_total, sums[1], sums[2], sums[3], sums[4], sums[5])
```

```python
import functools
import math

import jax
import jax.numpy as jnp
from jax import lax
from jax.experimental import pallas as pl
from jax.experimental.pallas import tpu as pltpu
from jax.sharding import PartitionSpec as P

STEPS = 128
LANES = 128
F32 = jnp.float32
BF16 = jnp.bfloat16
MESH = pl.DeviceIdType.MESH


def dot(a, b):
    return lax.dot_general(a, b, (((1,), (0,)), ((), ())), preferred_element_type=F32)


def dot_nt(a, b):
    return lax.dot_general(a, b, (((1,), (1,)), ((), ())), preferred_element_type=F32)


def dot_tn(a, b):
    return lax.dot_general(a, b, (((0,), (0,)), ((), ())), preferred_element_type=F32)


def later(values, by):
    row = lax.broadcasted_iota(jnp.int32, values.shape, 0)
    return jnp.where(row >= by, pltpu.roll(values, by, 0), 0.0)


def earlier(values, by):
    row = lax.broadcasted_iota(jnp.int32, values.shape, 0)
    return jnp.where(row < STEPS - by, pltpu.roll(values, STEPS - by, 0), 0.0)


def kernel(
    n, g, count,
    offs_ref, xq_ref, w1_ref, w2_ref, gain_ref, wc_ref, wp_ref,
    gs_ref, gc_ref, gp_ref, small_ref,
    hid, acc_a, acc_b, pre2, normed, inv, latent, context, pred, negs, negw, posq, qg, glat, cgv, pv, gfirst,
    panel, own_out, own_in, loss_acc, small_in, small_z,
    stage, core_in, chip_in, z_out, z_in, fin,
    panel_s, panel_r, own_s, own_r, sdp_s, sdp_r, sz_s, sz_r,
    core_s, core_r, chip_s, chip_r, z_s, z_r, f_s, f_r,
):
    tokens, channels = latent.shape
    wins = tokens // STEPS
    horizons = wp_ref.shape[0]
    pieces, _, chips, prow, _ = stage.shape
    picks = offs_ref.shape[0]
    per = picks // horizons
    cols = channels // g
    scale = 1.0 / math.sqrt(channels)
    me = lax.axis_index("dp")
    zme = lax.axis_index("grp")
    my_core = lax.rem(me, 2)
    my_chip = me // 2
    quarters = hid.shape[0]

    def dp_peer(j):
        return lax.rem(me + j, n)

    def z_peer(j):
        return lax.rem(zme + j, g)

    def chip_peer(j):
        return lax.rem(my_chip + j, chips)

    def each(size, body):
        def step(j, carry):
            body(j)
            return carry

        lax.fori_loop(1, size, step, 0)

    def windows(body):
        def step(w, carry):
            body(pl.ds(pl.multiple_of(w * STEPS, STEPS), STEPS))
            return carry

        lax.fori_loop(0, wins, step, 0)

    barrier = pltpu.get_barrier_semaphore()
    each(n, lambda j: pl.semaphore_signal(barrier, inc=1, device_id={"dp": dp_peer(j)}, device_id_type=MESH))
    each(g, lambda j: pl.semaphore_signal(barrier, inc=1, device_id={"grp": z_peer(j)}, device_id_type=MESH))

    def to_dp(src, dst, ssem, rsem, peer):
        return pltpu.make_async_remote_copy(
            src_ref=src, dst_ref=dst, send_sem=ssem, recv_sem=rsem, device_id={"dp": peer}, device_id_type=MESH
        )

    def to_z(src, dst, ssem, rsem, peer):
        return pltpu.make_async_remote_copy(
            src_ref=src, dst_ref=dst, send_sem=ssem, recv_sem=rsem, device_id={"grp": peer}, device_id_type=MESH
        )

    acc_a[...] = jnp.zeros_like(acc_a)
    acc_b[...] = jnp.zeros_like(acc_b)

    def quarter(q, carry):
        h = jnp.maximum(dot(xq_ref[q], w1_ref[...]), 0.0).astype(BF16)
        hid[q] = h
        acc_a[...] += dot(h, w2_ref[q])
        acc_b[...] += dot(h, w2_ref[q + quarters])
        return carry

    lax.fori_loop(0, quarters, quarter, 0)

    def norm(rows):
        pre = later(acc_a[rows, :], 1) + acc_b[rows, :]
        pre2[rows, :] = pre
        active = jnp.maximum(pre, 0.0)
        centred = active - jnp.mean(active, axis=1, keepdims=True)
        inv_std = lax.rsqrt(jnp.mean(centred * centred, axis=1, keepdims=True) + 1e-05)
        norm_row = centred * inv_std
        normed[rows, :] = norm_row
        inv[rows, :] = inv_std
        latent[rows, :] = (norm_row * gain_ref[...]).astype(BF16)

    windows(norm)

    place = lax.broadcasted_iota(jnp.int32, (picks, tokens), 1)
    chosen = jnp.where(place == offs_ref[...], 1.0, 0.0).astype(BF16)
    panel[me] = dot(chosen, latent[...]).astype(BF16)
    pl.semaphore_wait(barrier, n - 1 + g - 1)

    def panel_copy(j, slot):
        return to_dp(panel.at[slot], panel.at[slot], panel_s.at[j], panel_r.at[slot], dp_peer(j))

    each(n, lambda j: panel_copy(j, me).start())

    acc_a[...] = dot(latent[...], wc_ref[0])
    acc_b[...] = dot(latent[...], wc_ref[1])

    def make_context(rows):
        context[rows, :] = (later(acc_a[rows, :], 1) + acc_b[rows, :]).astype(BF16)

    windows(make_context)
    for k in range(horizons):
        pred[k] = dot(context[...], wp_ref[k]).astype(BF16)
    glat[...] = jnp.zeros_like(glat)
    loss_acc[...] = jnp.zeros_like(loss_acc)
    each(n, lambda j: panel_copy(j, dp_peer(j)).wait_recv())

    def panel_rows(k):
        return panel[:, k * per : (k + 1) * per, :].reshape(n * per, channels)

    for k in range(horizons):
        negs[...] = dot_nt(pred[k], panel_rows(k)) * scale

        def head(rows, k=k):
            query = pred[k, rows, :].astype(F32)
            target = earlier(latent[rows, :].astype(F32), k + 1)
            step = lax.broadcasted_iota(jnp.int32, (STEPS, 1), 0)
            valid = jnp.where(step + (k + 1) < STEPS, 1.0, 0.0)
            positive = jnp.sum(query * target, axis=1, keepdims=True) * scale
            negative = negs[rows, :]
            highest = jnp.maximum(positive, jnp.max(negative, axis=1, keepdims=True))
            denominator = jnp.exp(positive - highest) + jnp.sum(
                jnp.exp(negative - highest), axis=1, keepdims=True
            )
            log_total = highest + jnp.log(denominator)
            lost = jnp.sum(valid * (log_total - positive), axis=0, keepdims=True)
            loss_acc[...] += jnp.broadcast_to(lost, loss_acc.shape)
            pos_grad = valid * (jnp.exp(positive - log_total) - 1.0) * (scale / count)
            negw[k, rows, :] = (valid * jnp.exp(negative - log_total) * (scale / count)).astype(BF16)
            posq[k, rows, :] = pos_grad * target
            glat[rows, :] += later(pos_grad * query, k + 1)

        windows(head)
        owed = dot_tn(negw[k], pred[k]).astype(BF16)
        own_out[:, k * per : (k + 1) * per, :] = owed.reshape(n, per, channels)

    def own_copy(j, slot):
        return to_dp(own_out.at[dp_peer(j)], own_in.at[slot], own_s.at[j], own_r.at[slot], dp_peer(j))

    each(n, lambda j: own_copy(j, me).start())

    def core_copy(p):
        return to_dp(stage.at[p, 1 - my_core], core_in.at[p], core_s.at[p], core_r.at[p], me + 1 - 2 * my_core)

    def chip_copy(p, j, slot):
        c = chip_peer(j)
        return to_dp(
            stage.at[p, my_core, c], chip_in.at[p, slot], chip_s.at[p, j], chip_r.at[p, slot], c * 2 + my_core
        )

    def z_copy(p, j, slot):
        return to_z(z_out.at[p, z_peer(j)], z_in.at[p, slot], z_s.at[p, j], z_r.at[p, slot], z_peer(j))

    def fin_copy(p, j, slot):
        return to_z(fin.at[p, slot], fin.at[p, slot], f_s.at[p, j], f_r.at[p, slot], z_peer(j))

    def core_done(p):
        core_copy(p).wait_recv()

        def add(c, carry):
            total = stage[p, my_core, c].astype(F32) + core_in[p, c].astype(F32)
            stage[p, my_core, c] = total.astype(BF16)
            return carry

        lax.fori_loop(0, chips, add, 0)
        each(chips, lambda j: chip_copy(p, j, my_chip).start())

    def chip_done(p):
        each(chips, lambda j: chip_copy(p, j, chip_peer(j)).wait_recv())

        def add(j, total):
            return total + chip_in[p, chip_peer(j)].astype(F32)

        total = lax.fori_loop(1, chips, add, stage[p, my_core, my_chip].astype(F32)).astype(BF16)
        for z in range(g):
            z_out[p, z] = total[:, z * cols : (z + 1) * cols]
        each(g, lambda j: z_copy(p, j, zme).start())

    def z_done(p):
        each(g, lambda j: z_copy(p, j, z_peer(j)).wait_recv())

        def add(j, total):
            return total + z_in[p, z_peer(j)].astype(F32)

        fin[p, zme] = lax.fori_loop(1, g, add, z_out[p, zme].astype(F32)).astype(BF16)
        each(g, lambda j: fin_copy(p, j, zme).start())

    def fin_done(p):
        each(g, lambda j: fin_copy(p, j, z_peer(j)).wait_recv())
        for z in range(g):
            at = slice(z * cols, (z + 1) * cols)
            value = fin[p, z].astype(F32)
            if p == 0:
                part = prow // horizons
                for k in range(horizons):
                    gp_ref[k, :, at] = value[k * part : (k + 1) * part]
            elif p == 1:
                gc_ref[:, at] = value
            else:
                gs_ref[(p - 2) * prow : (p - 1) * prow, at] = value

    shares = []
    for k in range(horizons):
        qg[k] = (posq[k] + dot(negw[k], panel_rows(k))).astype(BF16)
        shares.append(dot_tn(context[...], qg[k]).reshape(n, channels // n, channels))
    joined = jnp.concatenate(shares, axis=1).astype(BF16).reshape(chips, 2, prow, channels)
    for parity in range(2):
        stage[0, parity] = joined[:, parity]
    core_copy(0).start()

    acc_a[...] = dot_nt(qg[0], wp_ref[0])
    for k in range(1, horizons):
        acc_a[...] += dot_nt(qg[k], wp_ref[k])

    def make_context_grad(rows):
        rounded = acc_a[rows, :].astype(BF16)
        cgv[1, rows, :] = rounded
        cgv[0, rows, :] = earlier(rounded.astype(F32), 1).astype(BF16)

    windows(make_context_grad)
    for half in range(2):
        share = dot_tn(latent[...], cgv[half]).astype(BF16).reshape(chips // 2, 2, prow, channels)
        for parity in range(2):
            stage[1, parity, half * (chips // 2) : (half + 1) * (chips // 2)] = share[:, parity]
    core_copy(1).start()
    acc_a[...] = dot_nt(cgv[1], wc_ref[1]) + dot_nt(cgv[0], wc_ref[0])

    each(n, lambda j: own_copy(j, dp_peer(j)).wait_recv())
    owned = lax.fori_loop(
        1, n, lambda j, total: total + own_in[dp_peer(j)].astype(F32), own_out[me].astype(F32)
    )
    high = owned.astype(BF16)
    low = (owned - high.astype(F32)).astype(BF16)
    acc_b[...] = dot_tn(chosen, high) + dot_tn(chosen, low)
    core_done(0)
    core_done(1)
    small_in[me] = jnp.zeros_like(small_in[me])
    gfirst[...] = jnp.zeros_like(gfirst)

    def norm_back(rows):
        total = glat[rows, :] + acc_a[rows, :] + acc_b[rows, :]
        norm_row = normed[rows, :]
        small_in[me, 0:1] += jnp.sum(total * norm_row, axis=0, keepdims=True)
        grad = total * gain_ref[...]
        active_grad = inv[rows, :] * (
            grad
            - jnp.mean(grad, axis=1, keepdims=True)
            - norm_row * jnp.mean(grad * norm_row, axis=1, keepdims=True)
        )
        rounded = jnp.where(pre2[rows, :] > 0, active_grad, 0.0).astype(BF16)
        pv[1, rows, :] = rounded
        pv[0, rows, :] = earlier(rounded.astype(F32), 1).astype(BF16)

    windows(norm_back)

    blocks = channels // LANES
    seconds = pieces - 2

    def second(b, i):
        lhs = hid[lax.rem(b, quarters), :, i * LANES : (i + 1) * LANES]
        return dot_tn(lhs, pv[b // quarters]).astype(BF16)

    if prow == LANES:
        for i in range(seconds):

            def fill(b, carry, i=i):
                stage[2 + i, lax.rem(b, 2), b // 2] = second(b, i)
                return carry

            lax.fori_loop(0, 2 * quarters, fill, 0)
            core_copy(2 + i).start()
            if i > 0:
                core_done(1 + i)
    else:
        each_chips = LANES // (seconds * prow) // 2

        def fill(b, carry):
            for i in range(blocks):
                share = second(b, i).reshape(each_chips, 2, seconds, prow, channels)
                at = pl.ds((b * blocks + i) * each_chips, each_chips)
                for parity in range(2):
                    for s in range(seconds):
                        stage[2 + s, parity, at] = share[:, parity, s]
            return carry

        lax.fori_loop(0, 2 * quarters, fill, 0)
        for i in range(seconds):
            core_copy(2 + i).start()
            if i > 0:
                core_done(1 + i)
    core_done(pieces - 1)
    chip_done(0)
    chip_done(1)

    def first(q, carry):
        back = dot_nt(pv[1], w2_ref[q + quarters]) + dot_nt(pv[0], w2_ref[q])
        pre = dot(xq_ref[q], w1_ref[...])
        gfirst[...] += dot_tn(xq_ref[q], jnp.where(pre > 0, back, 0.0).astype(BF16))
        return carry

    lax.fori_loop(0, quarters, first, 0)
    row = lax.broadcasted_iota(jnp.int32, (16, channels), 0)
    gain_row = small_in[me, 0:1]
    small_in[me] = (
        jnp.where(row < 10, gfirst[0:16, :], 0.0)
        + jnp.where(row == 10, gain_row, 0.0)
        + jnp.where(row == 11, loss_acc[...], 0.0)
    )

    def small_copy(j, slot):
        return to_dp(small_in.at[slot], small_in.at[slot], sdp_s.at[j], sdp_r.at[slot], dp_peer(j))

    def small_z_copy(j, slot):
        return to_z(small_z.at[slot], small_z.at[slot], sz_s.at[j], sz_r.at[slot], z_peer(j))

    each(n, lambda j: small_copy(j, me).start())
    chip_done(2)
    z_done(0)
    z_done(1)
    each(n, lambda j: small_copy(j, dp_peer(j)).wait_recv())
    small_z[zme] = lax.fori_loop(1, n, lambda j, total: total + small_in[j], small_in[0])
    each(g, lambda j: small_z_copy(j, zme).start())
    for p in range(3, pieces):
        chip_done(p)
        z_done(p - 1)
        fin_done(p - 3)
    z_done(pieces - 1)
    each(g, lambda j: small_z_copy(j, z_peer(j)).wait_recv())
    small_ref[...] = lax.fori_loop(1, g, lambda j, total: total + small_z[j], small_z[0])
    for p in range(pieces - 3, pieces):
        fin_done(p)

    def leave_dp(j):
        panel_copy(j, me).wait_send()
        own_copy(j, me).wait_send()
        small_copy(j, me).wait_send()

    each(n, leave_dp)
    each(g, lambda j: small_z_copy(j, zme).wait_send())
    for p in range(pieces):
        core_copy(p).wait_send()
        each(chips, lambda j, p=p: chip_copy(p, j, my_chip).wait_send())

        def leave_z(j, p=p):
            z_copy(p, j, zme).wait_send()
            fin_copy(p, j, zme).wait_send()

        each(g, leave_z)


def frame_inputs(audio_row, starts, channels):
    span = 20 * STEPS
    rows = []
    for w in range(starts.shape[0]):
        wave = lax.dynamic_slice_in_dim(audio_row, starts[w], span)
        steps = wave.reshape(STEPS, 20)
        before = jnp.concatenate([jnp.zeros((1, 5), wave.dtype), steps[:-1, 15:]], axis=0)
        rows.append(jnp.concatenate([before, steps], axis=1))
    wide = jnp.concatenate(rows, axis=0)
    parts = [jnp.pad(wide[:, 5 * q : 5 * q + 10], ((0, 0), (0, LANES - 10))) for q in range(4)]
    return jnp.stack(parts)


def on_device(audio, starts, offsets, w_first, w_second, gain, w_context, w_predict):
    channels = w_second.shape[1]
    horizons = w_predict.shape[0]
    g = lax.axis_size("grp")
    n = lax.axis_size("dp")
    wins = starts.shape[0]
    tokens = wins * STEPS
    count = float(wins * g * n * (horizons * STEPS - horizons * (horizons + 1) // 2))
    xq = frame_inputs(audio[0], starts, channels)
    w1 = jnp.pad(w_first, ((0, LANES - w_first.shape[0]), (0, 0)))
    picks = offsets.shape[1] * offsets.shape[2]
    offs = offsets.reshape(picks, 1)
    quarters = w_second.shape[0] // (2 * channels)
    prow = 2 * channels // n
    pieces = 2 + w_second.shape[0] // (2 * channels)
    chips = n // 2
    cols = channels // g
    panel_width = n * offsets.shape[2]
    vm = pltpu.VMEM
    dma = pltpu.SemaphoreType.DMA
    spec = pl.BlockSpec(memory_space=pltpu.VMEM)
    full = (tokens, channels)
    gs, gc, gp, small = pl.pallas_call(
        functools.partial(kernel, n, g, count),
        out_shape=(
            jax.ShapeDtypeStruct((w_second.shape[0] // n, channels), F32),
            jax.ShapeDtypeStruct((w_context.shape[0] // n, channels), F32),
            jax.ShapeDtypeStruct((horizons, channels // n, channels), F32),
            jax.ShapeDtypeStruct((16, channels), F32),
        ),
        in_specs=[spec] * 7,
        out_specs=[spec] * 4,
        scratch_shapes=[
            vm((quarters,) + full, BF16),
            vm(full, F32),
            vm(full, F32),
            vm(full, F32),
            vm(full, F32),
            vm((tokens, 1), F32),
            vm(full, BF16),
            vm(full, BF16),
            vm((horizons,) + full, BF16),
            vm((tokens, panel_width), F32),
            vm((horizons, tokens, panel_width), BF16),
            vm((horizons,) + full, F32),
            vm((horizons,) + full, BF16),
            vm(full, F32),
            vm((2,) + full, BF16),
            vm((2,) + full, BF16),
            vm((LANES, channels), F32),
            vm((n, picks, channels), BF16),
            vm((n, picks, channels), BF16),
            vm((n, picks, channels), BF16),
            vm((1, channels), F32),
            vm((n, 16, channels), F32),
            vm((g, 16, channels), F32),
            vm((pieces, 2, chips, prow, channels), BF16),
            vm((pieces, chips, prow, channels), BF16),
            vm((pieces, chips, prow, channels), BF16),
            vm((pieces, g, prow, cols), BF16),
            vm((pieces, g, prow, cols), BF16),
            vm((pieces, g, prow, cols), BF16),
        ]
        + [dma((n,))] * 6
        + [dma((g,))] * 2
        + [dma((pieces,))] * 2
        + [dma((pieces, chips))] * 2
        + [dma((pieces, g))] * 4,
        compiler_params=pltpu.CompilerParams(
            collective_id=0, has_side_effects=True, vmem_limit_bytes=56 * 1024 * 1024
        ),
    )(
        offs,
        xq,
        w1,
        w_second.reshape(2 * quarters, channels, channels),
        gain.reshape(1, channels),
        w_context.reshape(2, channels, channels),
        w_predict,
    )
    return (small[11, 0] / count, small[:10], gs, small[10], gc, gp)


def solution(mesh):
    return jax.shard_map(
        on_device,
        mesh=mesh,
        in_specs=(
            P(("grp", "dp"), None),
            P(("grp", "dp")),
            P(("grp", "dp"), None, None),
            P(),
            P(),
            P(),
            P(),
            P(),
        ),
        out_specs=(P(), P(), P("dp", None), P(), P("dp", None), P(None, "dp", None)),
        check_vma=False,
    )
```

```python
import functools
import math

import jax
import jax.numpy as jnp
from jax import lax
from jax.experimental import pallas as pl
from jax.experimental.pallas import tpu as pltpu
from jax.sharding import PartitionSpec as P

STEPS = 128
LANES = 128
F32 = jnp.float32
BF16 = jnp.bfloat16
MESH = pl.DeviceIdType.MESH


def dot(a, b):
    return lax.dot_general(a, b, (((1,), (0,)), ((), ())), preferred_element_type=F32)


def dot_nt(a, b):
    return lax.dot_general(a, b, (((1,), (1,)), ((), ())), preferred_element_type=F32)


def dot_tn(a, b):
    return lax.dot_general(a, b, (((0,), (0,)), ((), ())), preferred_element_type=F32)


def later(values, by):
    row = lax.broadcasted_iota(jnp.int32, values.shape, 0)
    return jnp.where(row >= by, pltpu.roll(values, by, 0), 0.0)


def earlier(values, by):
    row = lax.broadcasted_iota(jnp.int32, values.shape, 0)
    return jnp.where(row < STEPS - by, pltpu.roll(values, STEPS - by, 0), 0.0)


def kernel(
    n, g, count,
    offs_ref, x_ref, first_ref, w2_ref, gain_ref, wc_ref, wp_ref,
    fin, small_ref,
    w1, hid, acc_a, acc_b, pre2, normed, inv, latent, context, pred, negs, negw, posq, qg, glat, cgv, pv, gfirst, w1f,
    panel, own_out, own_in, loss_acc, small_in, small_z,
    stage, core_in, chip_in, z_out, z_in,
    panel_s, panel_r, own_s, own_r, sdp_s, sdp_r, sz_s, sz_r,
    core_s, core_r, chip_s, chip_r, z_s, z_r, f_s, f_r,
):
    tokens, channels = latent.shape
    wins = tokens // STEPS
    horizons = wp_ref.shape[0]
    pieces, _, chips, prow, _ = stage.shape
    per = offs_ref.shape[2]
    cols = channels // g
    scale = 1.0 / math.sqrt(channels)
    me = lax.axis_index("dp")
    zme = lax.axis_index("grp")
    my_core = lax.rem(me, 2)
    my_chip = me // 2
    quarters = hid.shape[0]

    def dp_peer(j):
        return lax.rem(me + j, n)

    def z_peer(j):
        return lax.rem(zme + j, g)

    def chip_peer(j):
        return lax.rem(my_chip + j, chips)

    def each(size, body):
        def step(j, carry):
            body(j)
            return carry

        lax.fori_loop(1, size, step, 0)

    def windows(body):
        def step(w, carry):
            body(pl.ds(pl.multiple_of(w * STEPS, STEPS), STEPS))
            return carry

        lax.fori_loop(0, wins, step, 0)

    barrier = pltpu.get_barrier_semaphore()
    each(n, lambda j: pl.semaphore_signal(barrier, inc=1, device_id={"dp": dp_peer(j)}, device_id_type=MESH))
    each(g, lambda j: pl.semaphore_signal(barrier, inc=1, device_id={"grp": z_peer(j)}, device_id_type=MESH))

    def to_dp(src, dst, ssem, rsem, peer):
        return pltpu.make_async_remote_copy(
            src_ref=src, dst_ref=dst, send_sem=ssem, recv_sem=rsem, device_id={"dp": peer}, device_id_type=MESH
        )

    def to_z(src, dst, ssem, rsem, peer):
        return pltpu.make_async_remote_copy(
            src_ref=src, dst_ref=dst, send_sem=ssem, recv_sem=rsem, device_id={"grp": peer}, device_id_type=MESH
        )

    taps = first_ref.shape[0]
    w1f[...] = jnp.zeros_like(w1f)
    for q in range(quarters):
        w1f[q, taps // 2 * q : taps // 2 * q + taps, :] = first_ref[...].astype(F32)
    w1[...] = w1f[...].astype(BF16)

    acc_a[...] = jnp.zeros_like(acc_a)
    acc_b[...] = jnp.zeros_like(acc_b)

    def quarter(q, carry):
        h = jnp.maximum(dot(x_ref[...], w1[q]), 0.0).astype(BF16)
        hid[q] = h
        acc_a[...] += dot(h, w2_ref[q])
        acc_b[...] += dot(h, w2_ref[q + quarters])
        return carry

    lax.fori_loop(0, quarters, quarter, 0)

    def norm(rows):
        pre = later(acc_a[rows, :], 1) + acc_b[rows, :]
        pre2[rows, :] = pre
        active = jnp.maximum(pre, 0.0)
        centred = active - jnp.mean(active, axis=1, keepdims=True)
        inv_std = lax.rsqrt(jnp.mean(centred * centred, axis=1, keepdims=True) + 1e-05)
        norm_row = centred * inv_std
        normed[rows, :] = norm_row
        inv[rows, :] = inv_std
        latent[rows, :] = (norm_row * gain_ref[...]).astype(BF16)

    windows(norm)

    place = lax.broadcasted_iota(jnp.int32, (tokens, per), 0)
    chosen = [jnp.where(place == offs_ref[0, k : k + 1, :], 1.0, 0.0).astype(BF16) for k in range(horizons)]
    for k in range(horizons):
        panel[me, k * per : (k + 1) * per] = dot_tn(chosen[k], latent[...]).astype(BF16)
    pl.semaphore_wait(barrier, n - 1 + g - 1)

    def panel_copy(j, slot):
        return to_dp(panel.at[slot], panel.at[slot], panel_s.at[j], panel_r.at[slot], dp_peer(j))

    each(n, lambda j: panel_copy(j, me).start())

    acc_a[...] = dot(latent[...], wc_ref[0])
    acc_b[...] = dot(latent[...], wc_ref[1])

    def make_context(rows):
        context[rows, :] = (later(acc_a[rows, :], 1) + acc_b[rows, :]).astype(BF16)

    windows(make_context)
    for k in range(horizons):
        pred[k] = dot(context[...], wp_ref[k]).astype(BF16)
    glat[...] = jnp.zeros_like(glat)
    loss_acc[...] = jnp.zeros_like(loss_acc)
    each(n, lambda j: panel_copy(j, dp_peer(j)).wait_recv())

    def panel_rows(k):
        return panel[:, k * per : (k + 1) * per, :].reshape(n * per, channels)

    for k in range(horizons):
        negs[...] = dot_nt(pred[k], panel_rows(k)) * scale

        def head(rows, k=k):
            query = pred[k, rows, :].astype(F32)
            target = earlier(latent[rows, :].astype(F32), k + 1)
            step = lax.broadcasted_iota(jnp.int32, (STEPS, 1), 0)
            valid = jnp.where(step + (k + 1) < STEPS, 1.0, 0.0)
            positive = jnp.sum(query * target, axis=1, keepdims=True) * scale
            negative = negs[rows, :]
            highest = jnp.maximum(positive, jnp.max(negative, axis=1, keepdims=True))
            denominator = jnp.exp(positive - highest) + jnp.sum(
                jnp.exp(negative - highest), axis=1, keepdims=True
            )
            log_total = highest + jnp.log(denominator)
            lost = jnp.sum(valid * (log_total - positive), axis=0, keepdims=True)
            loss_acc[...] += jnp.broadcast_to(lost, loss_acc.shape)
            pos_grad = valid * (jnp.exp(positive - log_total) - 1.0) * (scale / count)
            negw[k, rows, :] = (valid * jnp.exp(negative - log_total) * (scale / count)).astype(BF16)
            posq[k, rows, :] = pos_grad * target
            glat[rows, :] += later(pos_grad * query, k + 1)

        windows(head)
        owed = dot_tn(negw[k], pred[k]).astype(BF16)
        own_out[:, k * per : (k + 1) * per, :] = owed.reshape(n, per, channels)

    def own_copy(j, slot):
        return to_dp(own_out.at[dp_peer(j)], own_in.at[slot], own_s.at[j], own_r.at[slot], dp_peer(j))

    each(n, lambda j: own_copy(j, me).start())

    def core_copy(p):
        return to_dp(stage.at[p, 1 - my_core], core_in.at[p], core_s.at[p], core_r.at[p], me + 1 - 2 * my_core)

    def chip_copy(p, j, slot):
        c = chip_peer(j)
        return to_dp(
            stage.at[p, my_core, c], chip_in.at[p, slot], chip_s.at[p, j], chip_r.at[p, slot], c * 2 + my_core
        )

    def z_copy(p, j, slot):
        return to_z(z_out.at[p, z_peer(j)], z_in.at[p, slot], z_s.at[p, j], z_r.at[p, slot], z_peer(j))

    def fin_copy(p, j, slot):
        return to_z(fin.at[p, slot], fin.at[p, slot], f_s.at[p, j], f_r.at[p, slot], z_peer(j))

    def core_done(p):
        core_copy(p).wait_recv()

        def add(c, carry):
            total = stage[p, my_core, c].astype(F32) + core_in[p, c].astype(F32)
            stage[p, my_core, c] = total.astype(BF16)
            return carry

        lax.fori_loop(0, chips, add, 0)
        each(chips, lambda j: chip_copy(p, j, my_chip).start())

    def chip_done(p):
        each(chips, lambda j: chip_copy(p, j, chip_peer(j)).wait_recv())

        def add(j, total):
            return total + chip_in[p, chip_peer(j)].astype(F32)

        total = lax.fori_loop(1, chips, add, stage[p, my_core, my_chip].astype(F32)).astype(BF16)
        for z in range(g):
            z_out[p, z] = total[:, z * cols : (z + 1) * cols]
        each(g, lambda j: z_copy(p, j, zme).start())

    def z_done(p):
        each(g, lambda j: z_copy(p, j, z_peer(j)).wait_recv())

        def add(j, total):
            return total + z_in[p, z_peer(j)].astype(F32)

        fin[p, zme] = lax.fori_loop(1, g, add, z_out[p, zme].astype(F32)).astype(BF16)
        each(g, lambda j: fin_copy(p, j, zme).start())

    def fin_done(p):
        each(g, lambda j: fin_copy(p, j, z_peer(j)).wait_recv())

    shares = []
    for k in range(horizons):
        qg[k] = (posq[k] + dot(negw[k], panel_rows(k))).astype(BF16)
        shares.append(dot_tn(context[...], qg[k]).reshape(n, channels // n, channels))
    joined = jnp.concatenate(shares, axis=1).astype(BF16).reshape(chips, 2, prow, channels)
    for parity in range(2):
        stage[0, parity] = joined[:, parity]
    core_copy(0).start()

    acc_a[...] = dot_nt(qg[0], wp_ref[0])
    for k in range(1, horizons):
        acc_a[...] += dot_nt(qg[k], wp_ref[k])

    def make_context_grad(rows):
        rounded = acc_a[rows, :].astype(BF16)
        cgv[1, rows, :] = rounded
        cgv[0, rows, :] = earlier(rounded.astype(F32), 1).astype(BF16)

    windows(make_context_grad)
    for half in range(2):
        share = dot_tn(latent[...], cgv[half]).astype(BF16).reshape(chips // 2, 2, prow, channels)
        for parity in range(2):
            stage[1, parity, half * (chips // 2) : (half + 1) * (chips // 2)] = share[:, parity]
    core_copy(1).start()
    acc_a[...] = dot_nt(cgv[1], wc_ref[1]) + dot_nt(cgv[0], wc_ref[0])

    each(n, lambda j: own_copy(j, dp_peer(j)).wait_recv())
    owned = lax.fori_loop(
        1, n, lambda j, total: total + own_in[dp_peer(j)].astype(F32), own_out[me].astype(F32)
    )
    high = owned.astype(BF16)
    low = (owned - high.astype(F32)).astype(BF16)
    acc_b[...] = jnp.zeros_like(acc_b)
    for k in range(horizons):
        mine = slice(k * per, (k + 1) * per)
        acc_b[...] += dot(chosen[k], high[mine]) + dot(chosen[k], low[mine])
    core_done(0)
    core_done(1)
    small_in[me] = jnp.zeros_like(small_in[me])

    def norm_back(rows):
        total = glat[rows, :] + acc_a[rows, :] + acc_b[rows, :]
        norm_row = normed[rows, :]
        small_in[me, 0:1] += jnp.sum(total * norm_row, axis=0, keepdims=True)
        grad = total * gain_ref[...]
        active_grad = inv[rows, :] * (
            grad
            - jnp.mean(grad, axis=1, keepdims=True)
            - norm_row * jnp.mean(grad * norm_row, axis=1, keepdims=True)
        )
        rounded = jnp.where(pre2[rows, :] > 0, active_grad, 0.0).astype(BF16)
        pv[1, rows, :] = rounded
        pv[0, rows, :] = earlier(rounded.astype(F32), 1).astype(BF16)

    windows(norm_back)

    blocks = channels // LANES
    seconds = pieces - 2

    def second(b, i):
        lhs = hid[lax.rem(b, quarters), :, i * LANES : (i + 1) * LANES]
        return dot_tn(lhs, pv[b // quarters]).astype(BF16)

    if prow == LANES:
        for i in range(seconds):

            def fill(b, carry, i=i):
                stage[2 + i, lax.rem(b, 2), b // 2] = second(b, i)
                return carry

            lax.fori_loop(0, 2 * quarters, fill, 0)
            core_copy(2 + i).start()
            if i > 0:
                core_done(1 + i)
    else:
        each_chips = LANES // (seconds * prow) // 2

        def fill(b, carry):
            for i in range(blocks):
                share = second(b, i).reshape(each_chips, 2, seconds, prow, channels)
                at = pl.ds((b * blocks + i) * each_chips, each_chips)
                for parity in range(2):
                    for s in range(seconds):
                        stage[2 + s, parity, at] = share[:, parity, s]
            return carry

        lax.fori_loop(0, 2 * quarters, fill, 0)
        for i in range(seconds):
            core_copy(2 + i).start()
            if i > 0:
                core_done(1 + i)
    core_done(pieces - 1)
    chip_done(0)
    chip_done(1)

    def first(q, carry):
        back = dot_nt(pv[1], w2_ref[q + quarters]) + dot_nt(pv[0], w2_ref[q])
        pre = dot(x_ref[...], w1[q])
        gfirst[q] = dot_tn(x_ref[...], jnp.where(pre > 0, back, 0.0).astype(BF16))
        return carry

    lax.fori_loop(0, quarters, first, 0)
    row = lax.broadcasted_iota(jnp.int32, (16, channels), 0)
    gain_row = small_in[me, 0:1]
    first_sum = gfirst[0, 0:16, :]
    for q in range(1, quarters):
        first_sum = first_sum + gfirst[q, taps // 2 * q : taps // 2 * q + 16, :]
    small_in[me] = (
        jnp.where(row < 10, first_sum, 0.0)
        + jnp.where(row == 10, gain_row, 0.0)
        + jnp.where(row == 11, loss_acc[...], 0.0)
    )

    def small_copy(j, slot):
        return to_dp(small_in.at[slot], small_in.at[slot], sdp_s.at[j], sdp_r.at[slot], dp_peer(j))

    def small_z_copy(j, slot):
        return to_z(small_z.at[slot], small_z.at[slot], sz_s.at[j], sz_r.at[slot], z_peer(j))

    each(n, lambda j: small_copy(j, me).start())
    chip_done(2)
    z_done(0)
    z_done(1)
    each(n, lambda j: small_copy(j, dp_peer(j)).wait_recv())
    small_z[zme] = lax.fori_loop(1, n, lambda j, total: total + small_in[j], small_in[0])
    each(g, lambda j: small_z_copy(j, zme).start())
    for p in range(3, pieces):
        chip_done(p)
        z_done(p - 1)
        fin_done(p - 3)
    z_done(pieces - 1)
    each(g, lambda j: small_z_copy(j, z_peer(j)).wait_recv())
    small_ref[...] = lax.fori_loop(1, g, lambda j, total: total + small_z[j], small_z[0])
    for p in range(pieces - 3, pieces):
        fin_done(p)

    def leave_dp(j):
        panel_copy(j, me).wait_send()
        own_copy(j, me).wait_send()
        small_copy(j, me).wait_send()

    each(n, leave_dp)
    each(g, lambda j: small_z_copy(j, zme).wait_send())
    for p in range(pieces):
        core_copy(p).wait_send()
        each(chips, lambda j, p=p: chip_copy(p, j, my_chip).wait_send())

        def leave_z(j, p=p):
            z_copy(p, j, zme).wait_send()
            fin_copy(p, j, zme).wait_send()

        each(g, leave_z)


def finish(count, fin_ref, small_ref, loss_ref, gf_ref, gs_ref, gg_ref, gc_ref, gp_ref):
    pieces, g, prow, cols = fin_ref.shape
    horizons, part, _ = gp_ref.shape
    for z in range(g):
        at = slice(z * cols, (z + 1) * cols)
        value = fin_ref[0, z].astype(F32)
        for k in range(horizons):
            gp_ref[k, :, at] = value[k * part : (k + 1) * part]
        gc_ref[:, at] = fin_ref[1, z].astype(F32)
        for p in range(2, pieces):
            gs_ref[(p - 2) * prow : (p - 1) * prow, at] = fin_ref[p, z].astype(F32)
    gf_ref[...] = small_ref[0:10, :]
    gg_ref[...] = small_ref[10:11, :]
    loss_ref[...] = small_ref[11:12, 0:1] / count


def frame_inputs(audio, starts):
    span = 20 * STEPS
    rows = []
    for w in range(starts.shape[0]):
        wave = lax.dynamic_slice(
            audio, (jnp.int32(0), starts[w]), (1, span), allow_negative_indices=False
        )
        steps = wave.reshape(STEPS, 20)
        before = jnp.concatenate([jnp.zeros((1, 5), wave.dtype), steps[:-1, 15:]], axis=0)
        rows.append(jnp.concatenate([before, steps], axis=1))
    return jnp.pad(jnp.concatenate(rows, axis=0), ((0, 0), (0, LANES - 25)))


def on_device(audio, starts, offsets, w_first, w_second, gain, w_context, w_predict):
    channels = w_second.shape[1]
    horizons = w_predict.shape[0]
    g = lax.axis_size("grp")
    n = lax.axis_size("dp")
    wins = starts.shape[0]
    tokens = wins * STEPS
    count = float(wins * g * n * (horizons * STEPS - horizons * (horizons + 1) // 2))
    x = frame_inputs(audio, starts)
    picks = offsets.shape[1] * offsets.shape[2]
    quarters = w_second.shape[0] // (2 * channels)
    prow = 2 * channels // n
    pieces = 2 + w_second.shape[0] // (2 * channels)
    chips = n // 2
    cols = channels // g
    panel_width = n * offsets.shape[2]
    vm = pltpu.VMEM
    dma = pltpu.SemaphoreType.DMA
    spec = pl.BlockSpec(memory_space=pltpu.VMEM)
    full = (tokens, channels)
    fin, small = pl.pallas_call(
        functools.partial(kernel, n, g, count),
        out_shape=(
            jax.ShapeDtypeStruct((pieces, g, prow, cols), BF16),
            jax.ShapeDtypeStruct((16, channels), F32),
        ),
        in_specs=[spec] * 7,
        out_specs=[spec] * 2,
        scratch_shapes=[
            vm((quarters, LANES, channels), BF16),
            vm((quarters,) + full, BF16),
            vm(full, F32),
            vm(full, F32),
            vm(full, F32),
            vm(full, F32),
            vm((tokens, 1), F32),
            vm(full, BF16),
            vm(full, BF16),
            vm((horizons,) + full, BF16),
            vm((tokens, panel_width), F32),
            vm((horizons, tokens, panel_width), BF16),
            vm((horizons,) + full, F32),
            vm((horizons,) + full, BF16),
            vm(full, F32),
            vm((2,) + full, BF16),
            vm((2,) + full, BF16),
            vm((quarters, LANES, channels), F32),
            vm((quarters, LANES, channels), F32),
            vm((n, picks, channels), BF16),
            vm((n, picks, channels), BF16),
            vm((n, picks, channels), BF16),
            vm((1, channels), F32),
            vm((n, 16, channels), F32),
            vm((g, 16, channels), F32),
            vm((pieces, 2, chips, prow, channels), BF16),
            vm((pieces, chips, prow, channels), BF16),
            vm((pieces, chips, prow, channels), BF16),
            vm((pieces, g, prow, cols), BF16),
            vm((pieces, g, prow, cols), BF16),
        ]
        + [dma((n,))] * 6
        + [dma((g,))] * 2
        + [dma((pieces,))] * 2
        + [dma((pieces, chips))] * 2
        + [dma((pieces, g))] * 4,
        compiler_params=pltpu.CompilerParams(
            collective_id=0, has_side_effects=True, vmem_limit_bytes=56 * 1024 * 1024
        ),
    )(
        offsets,
        x,
        w_first,
        w_second.reshape(2 * quarters, channels, channels),
        gain.reshape(1, channels),
        w_context.reshape(2, channels, channels),
        w_predict,
    )
    loss, gf, gs, gg, gc, gp = pl.pallas_call(
        functools.partial(finish, count),
        out_shape=(
            jax.ShapeDtypeStruct((1, 1), F32),
            jax.ShapeDtypeStruct(w_first.shape, F32),
            jax.ShapeDtypeStruct((w_second.shape[0] // n, channels), F32),
            jax.ShapeDtypeStruct((1, channels), F32),
            jax.ShapeDtypeStruct((w_context.shape[0] // n, channels), F32),
            jax.ShapeDtypeStruct((horizons, channels // n, channels), F32),
        ),
        in_specs=[spec] * 2,
        out_specs=[spec] * 6,
    )(fin, small)
    return (loss.reshape(()), gf, gs, gg.reshape(channels), gc, gp)


def solution(mesh):
    return jax.shard_map(
        on_device,
        mesh=mesh,
        in_specs=(
            P(("grp", "dp"), None),
            P(("grp", "dp")),
            P(("grp", "dp"), None, None),
            P(),
            P(),
            P(),
            P(),
            P(),
        ),
        out_specs=(P(), P(), P("dp", None), P(), P("dp", None), P(None, "dp", None)),
        check_vma=False,
    )
```

```python
import functools
import math

import jax
import jax.numpy as jnp
from jax import lax
from jax.experimental import pallas as pl
from jax.experimental.pallas import tpu as pltpu
from jax.sharding import PartitionSpec as P

STEPS = 128
LANES = 128
F32 = jnp.float32
BF16 = jnp.bfloat16
MESH = pl.DeviceIdType.MESH


def dot(a, b):
    return lax.dot_general(a, b, (((1,), (0,)), ((), ())), preferred_element_type=F32)


def dot_nt(a, b):
    return lax.dot_general(a, b, (((1,), (1,)), ((), ())), preferred_element_type=F32)


def dot_tn(a, b):
    return lax.dot_general(a, b, (((0,), (0,)), ((), ())), preferred_element_type=F32)


def later(values, by):
    row = lax.broadcasted_iota(jnp.int32, values.shape, 0)
    return jnp.where(row >= by, pltpu.roll(values, by, 0), 0.0)


def earlier(values, by):
    row = lax.broadcasted_iota(jnp.int32, values.shape, 0)
    return jnp.where(row < STEPS - by, pltpu.roll(values, STEPS - by, 0), 0.0)


def kernel(
    n, g, count,
    offs_ref, x_ref, first_ref, w2_ref, gain_ref, wc_ref, wp_ref,
    fin, small_ref,
    w1, hid, acc_a, acc_b, pre2, normed, inv, latent, context, pred, negs, negw, posq, qg, glat, cgv, pv, gfirst, w1f,
    panel, own_out, own_in, loss_acc, small_in, small_z,
    stage, core_in, chip_in, z_out, z_in,
    panel_s, panel_r, own_s, own_r, sdp_s, sdp_r, sz_s, sz_r,
    core_s, core_r, chip_s, chip_r, z_s, z_r, f_s, f_r,
):
    tokens, channels = latent.shape
    wins = tokens // STEPS
    horizons = wp_ref.shape[0]
    pieces, _, chips, prow, _ = stage.shape
    per = offs_ref.shape[2]
    cols = channels // g
    scale = 1.0 / math.sqrt(channels)
    me = lax.axis_index("dp")
    zme = lax.axis_index("grp")
    my_core = lax.rem(me, 2)
    my_chip = me // 2
    quarters = hid.shape[0]

    def dp_peer(j):
        return lax.rem(me + j, n)

    def z_peer(j):
        return lax.rem(zme + j, g)

    def chip_peer(j):
        return lax.rem(my_chip + j, chips)

    def each(size, body):
        def step(j, carry):
            body(j)
            return carry

        lax.fori_loop(1, size, step, 0)

    def windows(body):
        def step(w, carry):
            body(pl.ds(pl.multiple_of(w * STEPS, STEPS), STEPS))
            return carry

        lax.fori_loop(0, wins, step, 0)

    barrier = pltpu.get_barrier_semaphore()
    each(n, lambda j: pl.semaphore_signal(barrier, inc=1, device_id={"dp": dp_peer(j)}, device_id_type=MESH))
    each(g, lambda j: pl.semaphore_signal(barrier, inc=1, device_id={"grp": z_peer(j)}, device_id_type=MESH))

    def to_dp(src, dst, ssem, rsem, peer):
        return pltpu.make_async_remote_copy(
            src_ref=src, dst_ref=dst, send_sem=ssem, recv_sem=rsem, device_id={"dp": peer}, device_id_type=MESH
        )

    def to_z(src, dst, ssem, rsem, peer):
        return pltpu.make_async_remote_copy(
            src_ref=src, dst_ref=dst, send_sem=ssem, recv_sem=rsem, device_id={"grp": peer}, device_id_type=MESH
        )

    taps = first_ref.shape[0]
    w1f[...] = jnp.zeros_like(w1f)
    for q in range(quarters):
        w1f[q, taps // 2 * q : taps // 2 * q + taps, :] = first_ref[...].astype(F32)
    w1[...] = w1f[...].astype(BF16)

    acc_a[...] = jnp.zeros_like(acc_a)
    acc_b[...] = jnp.zeros_like(acc_b)

    def quarter(q, carry):
        h = jnp.maximum(dot(x_ref[...], w1[q]), 0.0).astype(BF16)
        hid[q] = h
        acc_a[...] += dot(h, w2_ref[q])
        acc_b[...] += dot(h, w2_ref[q + quarters])
        return carry

    lax.fori_loop(0, quarters, quarter, 0)

    def norm(rows):
        pre = later(acc_a[rows, :], 1) + acc_b[rows, :]
        pre2[rows, :] = pre
        active = jnp.maximum(pre, 0.0)
        centred = active - jnp.mean(active, axis=1, keepdims=True)
        inv_std = lax.rsqrt(jnp.mean(centred * centred, axis=1, keepdims=True) + 1e-05)
        norm_row = centred * inv_std
        normed[rows, :] = norm_row
        inv[rows, :] = inv_std
        latent[rows, :] = (norm_row * gain_ref[...]).astype(BF16)

    windows(norm)

    place = lax.broadcasted_iota(jnp.int32, (tokens, per), 0)
    chosen = [jnp.where(place == offs_ref[0, k : k + 1, :], 1.0, 0.0).astype(BF16) for k in range(horizons)]
    for k in range(horizons):
        panel[me, k * per : (k + 1) * per] = dot_tn(chosen[k], latent[...]).astype(BF16)
    pl.semaphore_wait(barrier, n - 1 + g - 1)

    def panel_copy(j, slot):
        return to_dp(panel.at[slot], panel.at[slot], panel_s.at[j], panel_r.at[slot], dp_peer(j))

    each(n, lambda j: panel_copy(j, me).start())

    acc_a[...] = dot(latent[...], wc_ref[0])
    acc_b[...] = dot(latent[...], wc_ref[1])

    def make_context(rows):
        context[rows, :] = (later(acc_a[rows, :], 1) + acc_b[rows, :]).astype(BF16)

    windows(make_context)
    for k in range(horizons):
        pred[k] = dot(context[...], wp_ref[k]).astype(BF16)
    glat[...] = jnp.zeros_like(glat)
    loss_acc[...] = jnp.zeros_like(loss_acc)
    each(n, lambda j: panel_copy(j, dp_peer(j)).wait_recv())

    def panel_rows(k):
        return panel[:, k * per : (k + 1) * per, :].reshape(n * per, channels)

    for k in range(horizons):
        negs[...] = dot_nt(pred[k], panel_rows(k)) * scale

        def head(rows, k=k):
            query = pred[k, rows, :].astype(F32)
            target = earlier(latent[rows, :].astype(F32), k + 1)
            step = lax.broadcasted_iota(jnp.int32, (STEPS, 1), 0)
            valid = jnp.where(step + (k + 1) < STEPS, 1.0, 0.0)
            positive = jnp.sum(query * target, axis=1, keepdims=True) * scale
            negative = negs[rows, :]
            highest = jnp.maximum(positive, jnp.max(negative, axis=1, keepdims=True))
            denominator = jnp.exp(positive - highest) + jnp.sum(
                jnp.exp(negative - highest), axis=1, keepdims=True
            )
            log_total = highest + jnp.log(denominator)
            lost = jnp.sum(valid * (log_total - positive), axis=0, keepdims=True)
            loss_acc[...] += jnp.broadcast_to(lost, loss_acc.shape)
            pos_grad = valid * (jnp.exp(positive - log_total) - 1.0) * (scale / count)
            negw[k, rows, :] = (valid * jnp.exp(negative - log_total) * (scale / count)).astype(BF16)
            posq[k, rows, :] = pos_grad * target
            glat[rows, :] += later(pos_grad * query, k + 1)

        windows(head)
        owed = dot_tn(negw[k], pred[k]).astype(BF16)
        own_out[:, k * per : (k + 1) * per, :] = owed.reshape(n, per, channels)

    def own_copy(j, slot):
        return to_dp(own_out.at[dp_peer(j)], own_in.at[slot], own_s.at[j], own_r.at[slot], dp_peer(j))

    each(n, lambda j: own_copy(j, me).start())

    def core_copy(p):
        return to_dp(stage.at[p, 1 - my_core], core_in.at[p], core_s.at[p], core_r.at[p], me + 1 - 2 * my_core)

    def chip_copy(p, j, slot):
        c = chip_peer(j)
        return to_dp(
            stage.at[p, my_core, c], chip_in.at[p, slot], chip_s.at[p, j], chip_r.at[p, slot], c * 2 + my_core
        )

    def z_copy(p, j, slot):
        return to_z(z_out.at[p, z_peer(j)], z_in.at[p, slot], z_s.at[p, j], z_r.at[p, slot], z_peer(j))

    def fin_copy(p, j, slot):
        return to_z(fin.at[p, slot], fin.at[p, slot], f_s.at[p, j], f_r.at[p, slot], z_peer(j))

    def core_done(p):
        core_copy(p).wait_recv()

        def add(c, carry):
            total = stage[p, my_core, c].astype(F32) + core_in[p, c].astype(F32)
            stage[p, my_core, c] = total.astype(BF16)
            return carry

        lax.fori_loop(0, chips, add, 0)
        each(chips, lambda j: chip_copy(p, j, my_chip).start())

    def chip_done(p):
        each(chips, lambda j: chip_copy(p, j, chip_peer(j)).wait_recv())

        def add(j, total):
            return total + chip_in[p, chip_peer(j)].astype(F32)

        total = lax.fori_loop(1, chips, add, stage[p, my_core, my_chip].astype(F32)).astype(BF16)
        for z in range(g):
            z_out[p, z] = total[:, z * cols : (z + 1) * cols]
        each(g, lambda j: z_copy(p, j, zme).start())

    def z_done(p):
        each(g, lambda j: z_copy(p, j, z_peer(j)).wait_recv())

        def add(j, total):
            return total + z_in[p, z_peer(j)].astype(F32)

        fin[p, zme] = lax.fori_loop(1, g, add, z_out[p, zme].astype(F32)).astype(BF16)
        each(g, lambda j: fin_copy(p, j, zme).start())

    def fin_done(p):
        each(g, lambda j: fin_copy(p, j, z_peer(j)).wait_recv())

    shares = []
    for k in range(horizons):
        qg[k] = (posq[k] + dot(negw[k], panel_rows(k))).astype(BF16)
        shares.append(dot_tn(context[...], qg[k]).reshape(n, channels // n, channels))
    joined = jnp.concatenate(shares, axis=1).astype(BF16).reshape(chips, 2, prow, channels)
    for parity in range(2):
        stage[0, parity] = joined[:, parity]
    core_copy(0).start()

    acc_a[...] = dot_nt(qg[0], wp_ref[0])
    for k in range(1, horizons):
        acc_a[...] += dot_nt(qg[k], wp_ref[k])

    def make_context_grad(rows):
        rounded = acc_a[rows, :].astype(BF16)
        cgv[1, rows, :] = rounded
        cgv[0, rows, :] = earlier(rounded.astype(F32), 1).astype(BF16)

    windows(make_context_grad)
    for half in range(2):
        share = dot_tn(latent[...], cgv[half]).astype(BF16).reshape(chips // 2, 2, prow, channels)
        for parity in range(2):
            stage[1, parity, half * (chips // 2) : (half + 1) * (chips // 2)] = share[:, parity]
    core_copy(1).start()
    core_done(0)
    acc_a[...] = dot_nt(cgv[1], wc_ref[1]) + dot_nt(cgv[0], wc_ref[0])

    each(n, lambda j: own_copy(j, dp_peer(j)).wait_recv())
    owned = lax.fori_loop(
        1, n, lambda j, total: total + own_in[dp_peer(j)].astype(F32), own_out[me].astype(F32)
    )
    high = owned.astype(BF16)
    low = (owned - high.astype(F32)).astype(BF16)
    acc_b[...] = jnp.zeros_like(acc_b)
    for k in range(horizons):
        mine = slice(k * per, (k + 1) * per)
        acc_b[...] += dot(chosen[k], high[mine]) + dot(chosen[k], low[mine])
    core_done(1)
    small_in[me] = jnp.zeros_like(small_in[me])

    def norm_back(rows):
        total = glat[rows, :] + acc_a[rows, :] + acc_b[rows, :]
        norm_row = normed[rows, :]
        small_in[me, 0:1] += jnp.sum(total * norm_row, axis=0, keepdims=True)
        grad = total * gain_ref[...]
        active_grad = inv[rows, :] * (
            grad
            - jnp.mean(grad, axis=1, keepdims=True)
            - norm_row * jnp.mean(grad * norm_row, axis=1, keepdims=True)
        )
        rounded = jnp.where(pre2[rows, :] > 0, active_grad, 0.0).astype(BF16)
        pv[1, rows, :] = rounded
        pv[0, rows, :] = earlier(rounded.astype(F32), 1).astype(BF16)

    windows(norm_back)

    blocks = channels // LANES
    seconds = pieces - 2

    def second(b, i):
        lhs = hid[lax.rem(b, quarters), :, i * LANES : (i + 1) * LANES]
        return dot_tn(lhs, pv[b // quarters]).astype(BF16)

    if prow == LANES:
        for i in range(seconds):

            def fill(b, carry, i=i):
                stage[2 + i, lax.rem(b, 2), b // 2] = second(b, i)
                return carry

            lax.fori_loop(0, 2 * quarters, fill, 0)
            core_copy(2 + i).start()
            if i > 0:
                core_done(1 + i)
    else:
        each_chips = LANES // (seconds * prow) // 2

        def fill(b, carry):
            for i in range(blocks):
                share = second(b, i).reshape(each_chips, 2, seconds, prow, channels)
                at = pl.ds((b * blocks + i) * each_chips, each_chips)
                for parity in range(2):
                    for s in range(seconds):
                        stage[2 + s, parity, at] = share[:, parity, s]
            return carry

        lax.fori_loop(0, 2 * quarters, fill, 0)
        for i in range(seconds):
            core_copy(2 + i).start()
            if i > 0:
                core_done(1 + i)
    core_done(pieces - 1)
    chip_done(0)
    chip_done(1)

    def first(q, carry):
        back = dot_nt(pv[1], w2_ref[q + quarters]) + dot_nt(pv[0], w2_ref[q])
        pre = dot(x_ref[...], w1[q])
        gfirst[q] = dot_tn(x_ref[...], jnp.where(pre > 0, back, 0.0).astype(BF16))
        return carry

    lax.fori_loop(0, quarters, first, 0)
    chip_done(2)
    row = lax.broadcasted_iota(jnp.int32, (16, channels), 0)
    gain_row = small_in[me, 0:1]
    first_sum = gfirst[0, 0:16, :]
    for q in range(1, quarters):
        first_sum = first_sum + gfirst[q, taps // 2 * q : taps // 2 * q + 16, :]
    small_in[me] = (
        jnp.where(row < 10, first_sum, 0.0)
        + jnp.where(row == 10, gain_row, 0.0)
        + jnp.where(row == 11, loss_acc[...], 0.0)
    )

    def small_copy(j, slot):
        return to_dp(small_in.at[slot], small_in.at[slot], sdp_s.at[j], sdp_r.at[slot], dp_peer(j))

    def small_z_copy(j, slot):
        return to_z(small_z.at[slot], small_z.at[slot], sz_s.at[j], sz_r.at[slot], z_peer(j))

    each(n, lambda j: small_copy(j, me).start())
    z_done(0)
    z_done(1)
    for p in range(3, pieces):
        chip_done(p)
        z_done(p - 1)
    each(n, lambda j: small_copy(j, dp_peer(j)).wait_recv())
    small_z[zme] = lax.fori_loop(1, n, lambda j, total: total + small_in[j], small_in[0])
    each(g, lambda j: small_z_copy(j, zme).start())
    z_done(pieces - 1)
    each(g, lambda j: small_z_copy(j, z_peer(j)).wait_recv())
    small_ref[...] = lax.fori_loop(1, g, lambda j, total: total + small_z[j], small_z[0])
    for p in range(pieces):
        fin_done(p)

    def leave_dp(j):
        panel_copy(j, me).wait_send()
        own_copy(j, me).wait_send()
        small_copy(j, me).wait_send()

    each(n, leave_dp)
    each(g, lambda j: small_z_copy(j, zme).wait_send())
    for p in range(pieces):
        core_copy(p).wait_send()
        each(chips, lambda j, p=p: chip_copy(p, j, my_chip).wait_send())

        def leave_z(j, p=p):
            z_copy(p, j, zme).wait_send()
            fin_copy(p, j, zme).wait_send()

        each(g, leave_z)


def finish(count, fin_ref, small_ref, loss_ref, gf_ref, gs_ref, gg_ref, gc_ref, gp_ref):
    pieces, g, prow, cols = fin_ref.shape
    horizons, part, _ = gp_ref.shape
    for z in range(g):
        at = slice(z * cols, (z + 1) * cols)
        value = fin_ref[0, z].astype(F32)
        for k in range(horizons):
            gp_ref[k, :, at] = value[k * part : (k + 1) * part]
        gc_ref[:, at] = fin_ref[1, z].astype(F32)
        for p in range(2, pieces):
            gs_ref[(p - 2) * prow : (p - 1) * prow, at] = fin_ref[p, z].astype(F32)
    gf_ref[...] = small_ref[0:10, :]
    gg_ref[...] = small_ref[10:11, :]
    loss_ref[...] = small_ref[11:12, 0:1] / count


def frame_inputs(audio, starts):
    span = 20 * STEPS
    rows = []
    for w in range(starts.shape[0]):
        wave = lax.dynamic_slice(
            audio, (jnp.int32(0), starts[w]), (1, span), allow_negative_indices=False
        )
        steps = wave.reshape(STEPS, 20)
        before = jnp.concatenate([jnp.zeros((1, 5), wave.dtype), steps[:-1, 15:]], axis=0)
        rows.append(jnp.concatenate([before, steps], axis=1))
    return jnp.pad(jnp.concatenate(rows, axis=0), ((0, 0), (0, LANES - 25)))


def on_device(audio, starts, offsets, w_first, w_second, gain, w_context, w_predict):
    channels = w_second.shape[1]
    horizons = w_predict.shape[0]
    g = lax.axis_size("grp")
    n = lax.axis_size("dp")
    wins = starts.shape[0]
    tokens = wins * STEPS
    count = float(wins * g * n * (horizons * STEPS - horizons * (horizons + 1) // 2))
    x = frame_inputs(audio, starts)
    picks = offsets.shape[1] * offsets.shape[2]
    quarters = w_second.shape[0] // (2 * channels)
    prow = 2 * channels // n
    pieces = 2 + w_second.shape[0] // (2 * channels)
    chips = n // 2
    cols = channels // g
    panel_width = n * offsets.shape[2]
    vm = pltpu.VMEM
    dma = pltpu.SemaphoreType.DMA
    spec = pl.BlockSpec(memory_space=pltpu.VMEM)
    full = (tokens, channels)
    fin, small = pl.pallas_call(
        functools.partial(kernel, n, g, count),
        out_shape=(
            jax.ShapeDtypeStruct((pieces, g, prow, cols), BF16),
            jax.ShapeDtypeStruct((16, channels), F32),
        ),
        in_specs=[spec] * 7,
        out_specs=[spec] * 2,
        scratch_shapes=[
            vm((quarters, LANES, channels), BF16),
            vm((quarters,) + full, BF16),
            vm(full, F32),
            vm(full, F32),
            vm(full, F32),
            vm(full, F32),
            vm((tokens, 1), F32),
            vm(full, BF16),
            vm(full, BF16),
            vm((horizons,) + full, BF16),
            vm((tokens, panel_width), F32),
            vm((horizons, tokens, panel_width), BF16),
            vm((horizons,) + full, F32),
            vm((horizons,) + full, BF16),
            vm(full, F32),
            vm((2,) + full, BF16),
            vm((2,) + full, BF16),
            vm((quarters, LANES, channels), F32),
            vm((quarters, LANES, channels), F32),
            vm((n, picks, channels), BF16),
            vm((n, picks, channels), BF16),
            vm((n, picks, channels), BF16),
            vm((1, channels), F32),
            vm((n, 16, channels), F32),
            vm((g, 16, channels), F32),
            vm((pieces, 2, chips, prow, channels), BF16),
            vm((pieces, chips, prow, channels), BF16),
            vm((pieces, chips, prow, channels), BF16),
            vm((pieces, g, prow, cols), BF16),
            vm((pieces, g, prow, cols), BF16),
        ]
        + [dma((n,))] * 6
        + [dma((g,))] * 2
        + [dma((pieces,))] * 2
        + [dma((pieces, chips))] * 2
        + [dma((pieces, g))] * 4,
        compiler_params=pltpu.CompilerParams(
            collective_id=0, has_side_effects=True, vmem_limit_bytes=56 * 1024 * 1024
        ),
    )(
        offsets,
        x,
        w_first,
        w_second.reshape(2 * quarters, channels, channels),
        gain.reshape(1, channels),
        w_context.reshape(2, channels, channels),
        w_predict,
    )
    loss, gf, gs, gg, gc, gp = pl.pallas_call(
        functools.partial(finish, count),
        out_shape=(
            jax.ShapeDtypeStruct((1, 1), F32),
            jax.ShapeDtypeStruct(w_first.shape, F32),
            jax.ShapeDtypeStruct((w_second.shape[0] // n, channels), F32),
            jax.ShapeDtypeStruct((1, channels), F32),
            jax.ShapeDtypeStruct((w_context.shape[0] // n, channels), F32),
            jax.ShapeDtypeStruct((horizons, channels // n, channels), F32),
        ),
        in_specs=[spec] * 2,
        out_specs=[spec] * 6,
    )(fin, small)
    return (loss.reshape(()), gf, gs, gg.reshape(channels), gc, gp)


def solution(mesh):
    return jax.shard_map(
        on_device,
        mesh=mesh,
        in_specs=(
            P(("grp", "dp"), None),
            P(("grp", "dp")),
            P(("grp", "dp"), None, None),
            P(),
            P(),
            P(),
            P(),
            P(),
        ),
        out_specs=(P(), P(), P("dp", None), P(), P("dp", None), P(None, "dp", None)),
        check_vma=False,
    )
```

```python
import functools
import math

import jax
import jax.numpy as jnp
from jax import lax
from jax.experimental import pallas as pl
from jax.experimental.pallas import tpu as pltpu
from jax.sharding import PartitionSpec as P

STEPS = 128
LANES = 128
F32 = jnp.float32
BF16 = jnp.bfloat16
MESH = pl.DeviceIdType.MESH


def dot(a, b):
    return lax.dot_general(a, b, (((1,), (0,)), ((), ())), preferred_element_type=F32)


def dot_nt(a, b):
    return lax.dot_general(a, b, (((1,), (1,)), ((), ())), preferred_element_type=F32)


def dot_tn(a, b):
    return lax.dot_general(a, b, (((0,), (0,)), ((), ())), preferred_element_type=F32)


def later(values, by):
    row = lax.broadcasted_iota(jnp.int32, values.shape, 0)
    return jnp.where(row >= by, pltpu.roll(values, by, 0), 0.0)


def earlier(values, by):
    row = lax.broadcasted_iota(jnp.int32, values.shape, 0)
    return jnp.where(row < STEPS - by, pltpu.roll(values, STEPS - by, 0), 0.0)


def kernel(
    n, g, count,
    offs_ref, x_ref, first_ref, w2_ref, gain_ref, wc_ref, wp_ref,
    fin, small_ref,
    w1, hid, acc_a, acc_b, pre2, normed, inv, latent, context, pred, negs, negw, posq, qg, glat, cgv, pv, gfirst, w1f,
    panel, own_out, own_in, loss_acc, small_in, small_z,
    stage, core_in, chip_in, z_out, z_in,
    panel_s, panel_r, own_s, own_r, sdp_s, sdp_r, sz_s, sz_r,
    core_s, core_r, chip_s, chip_r, z_s, z_r, f_s, f_r,
):
    tokens, channels = latent.shape
    wins = tokens // STEPS
    horizons = wp_ref.shape[0]
    pieces, _, chips, prow, _ = stage.shape
    per = offs_ref.shape[2]
    cols = channels // g
    scale = 1.0 / math.sqrt(channels)
    me = lax.axis_index("dp")
    zme = lax.axis_index("grp")
    my_core = lax.rem(me, 2)
    my_chip = me // 2
    quarters = hid.shape[0]

    def dp_peer(j):
        return lax.rem(me + j, n)

    def z_peer(j):
        return lax.rem(zme + j, g)

    def chip_peer(j):
        return lax.rem(my_chip + j, chips)

    def each(size, body):
        def step(j, carry):
            body(j)
            return carry

        lax.fori_loop(1, size, step, 0)

    def windows(body):
        def step(w, carry):
            body(pl.ds(pl.multiple_of(w * STEPS, STEPS), STEPS))
            return carry

        lax.fori_loop(0, wins, step, 0)

    barrier = pltpu.get_barrier_semaphore()
    each(n, lambda j: pl.semaphore_signal(barrier, inc=1, device_id={"dp": dp_peer(j)}, device_id_type=MESH))
    each(g, lambda j: pl.semaphore_signal(barrier, inc=1, device_id={"grp": z_peer(j)}, device_id_type=MESH))

    def to_dp(src, dst, ssem, rsem, peer):
        return pltpu.make_async_remote_copy(
            src_ref=src, dst_ref=dst, send_sem=ssem, recv_sem=rsem, device_id={"dp": peer}, device_id_type=MESH
        )

    def to_z(src, dst, ssem, rsem, peer):
        return pltpu.make_async_remote_copy(
            src_ref=src, dst_ref=dst, send_sem=ssem, recv_sem=rsem, device_id={"grp": peer}, device_id_type=MESH
        )

    taps = first_ref.shape[0]
    w1f[...] = jnp.zeros_like(w1f)
    for q in range(quarters):
        w1f[q, taps // 2 * q : taps // 2 * q + taps, :] = first_ref[...].astype(F32)
    w1[...] = w1f[...].astype(BF16)

    acc_a[...] = jnp.zeros_like(acc_a)
    acc_b[...] = jnp.zeros_like(acc_b)

    def quarter(q, carry):
        h = jnp.maximum(dot(x_ref[...], w1[q]), 0.0).astype(BF16)
        hid[q] = h
        acc_a[...] += dot(h, w2_ref[q])
        acc_b[...] += dot(h, w2_ref[q + quarters])
        return carry

    lax.fori_loop(0, quarters, quarter, 0)

    def norm(rows):
        pre = later(acc_a[rows, :], 1) + acc_b[rows, :]
        pre2[rows, :] = pre
        active = jnp.maximum(pre, 0.0)
        centred = active - jnp.mean(active, axis=1, keepdims=True)
        inv_std = lax.rsqrt(jnp.mean(centred * centred, axis=1, keepdims=True) + 1e-05)
        norm_row = centred * inv_std
        normed[rows, :] = norm_row
        inv[rows, :] = inv_std
        latent[rows, :] = (norm_row * gain_ref[...]).astype(BF16)

    windows(norm)

    place = lax.broadcasted_iota(jnp.int32, (tokens, per), 0)
    chosen = [jnp.where(place == offs_ref[0, k : k + 1, :], 1.0, 0.0).astype(BF16) for k in range(horizons)]
    for k in range(horizons):
        panel[me, k * per : (k + 1) * per] = dot_tn(chosen[k], latent[...]).astype(BF16)
    pl.semaphore_wait(barrier, n - 1 + g - 1)

    def panel_copy(j, slot):
        return to_dp(panel.at[slot], panel.at[slot], panel_s.at[j], panel_r.at[slot], dp_peer(j))

    each(n, lambda j: panel_copy(j, me).start())

    acc_a[...] = dot(latent[...], wc_ref[0])
    acc_b[...] = dot(latent[...], wc_ref[1])

    def make_context(rows):
        context[rows, :] = (later(acc_a[rows, :], 1) + acc_b[rows, :]).astype(BF16)

    windows(make_context)
    for k in range(horizons):
        pred[k] = dot(context[...], wp_ref[k]).astype(BF16)
    glat[...] = jnp.zeros_like(glat)
    loss_acc[...] = jnp.zeros_like(loss_acc)
    each(n, lambda j: panel_copy(j, dp_peer(j)).wait_recv())

    def panel_rows(k):
        return panel[:, k * per : (k + 1) * per, :].reshape(n * per, channels)

    for k in range(horizons):
        negs[...] = dot_nt(pred[k], panel_rows(k)) * scale

        def head(rows, k=k):
            query = pred[k, rows, :].astype(F32)
            target = earlier(latent[rows, :].astype(F32), k + 1)
            step = lax.broadcasted_iota(jnp.int32, (STEPS, 1), 0)
            valid = jnp.where(step + (k + 1) < STEPS, 1.0, 0.0)
            positive = jnp.sum(query * target, axis=1, keepdims=True) * scale
            negative = negs[rows, :]
            highest = jnp.maximum(positive, jnp.max(negative, axis=1, keepdims=True))
            denominator = jnp.exp(positive - highest) + jnp.sum(
                jnp.exp(negative - highest), axis=1, keepdims=True
            )
            log_total = highest + jnp.log(denominator)
            lost = jnp.sum(valid * (log_total - positive), axis=0, keepdims=True)
            loss_acc[...] += jnp.broadcast_to(lost, loss_acc.shape)
            pos_grad = valid * (jnp.exp(positive - log_total) - 1.0) * (scale / count)
            negw[k, rows, :] = (valid * jnp.exp(negative - log_total) * (scale / count)).astype(BF16)
            posq[k, rows, :] = pos_grad * target
            glat[rows, :] += later(pos_grad * query, k + 1)

        windows(head)
        owed = dot_tn(negw[k], pred[k]).astype(BF16)
        own_out[:, k * per : (k + 1) * per, :] = owed.reshape(n, per, channels)

    def own_copy(j, slot):
        return to_dp(own_out.at[dp_peer(j)], own_in.at[slot], own_s.at[j], own_r.at[slot], dp_peer(j))

    each(n, lambda j: own_copy(j, me).start())

    def core_copy(p):
        return to_dp(stage.at[p, 1 - my_core], core_in.at[p], core_s.at[p], core_r.at[p], me + 1 - 2 * my_core)

    def chip_copy(p, j, slot):
        c = chip_peer(j)
        return to_dp(
            stage.at[p, my_core, c], chip_in.at[p, slot], chip_s.at[p, j], chip_r.at[p, slot], c * 2 + my_core
        )

    def z_copy(p, j, slot):
        return to_z(z_out.at[p, z_peer(j)], z_in.at[p, slot], z_s.at[p, j], z_r.at[p, slot], z_peer(j))

    def fin_copy(p, j, slot):
        return to_z(fin.at[p, slot], fin.at[p, slot], f_s.at[p, j], f_r.at[p, slot], z_peer(j))

    def core_done(p):
        core_copy(p).wait_recv()

        def add(c, carry):
            total = stage[p, my_core, c].astype(F32) + core_in[p, c].astype(F32)
            stage[p, my_core, c] = total.astype(BF16)
            return carry

        lax.fori_loop(0, chips, add, 0)
        each(chips, lambda j: chip_copy(p, j, my_chip).start())

    def chip_done(p):
        each(chips, lambda j: chip_copy(p, j, chip_peer(j)).wait_recv())

        def add(j, total):
            return total + chip_in[p, chip_peer(j)].astype(F32)

        total = lax.fori_loop(1, chips, add, stage[p, my_core, my_chip].astype(F32)).astype(BF16)
        for z in range(g):
            z_out[p, z] = total[:, z * cols : (z + 1) * cols]
        each(g, lambda j: z_copy(p, j, zme).start())

    def z_done(p):
        each(g, lambda j: z_copy(p, j, z_peer(j)).wait_recv())

        def add(j, total):
            return total + z_in[p, z_peer(j)].astype(F32)

        fin[p, zme] = lax.fori_loop(1, g, add, z_out[p, zme].astype(F32)).astype(BF16)
        each(g, lambda j: fin_copy(p, j, zme).start())

    def fin_done(p):
        each(g, lambda j: fin_copy(p, j, z_peer(j)).wait_recv())

    shares = []
    turned_context = context[...].T
    for k in range(horizons):
        qg[k] = (posq[k] + dot(negw[k], panel_rows(k))).astype(BF16)
        shares.append(dot(turned_context, qg[k]).reshape(n, channels // n, channels))
    joined = jnp.concatenate(shares, axis=1).astype(BF16).reshape(chips, 2, prow, channels)
    for parity in range(2):
        stage[0, parity] = joined[:, parity]
    core_copy(0).start()

    acc_a[...] = dot_nt(qg[0], wp_ref[0])
    for k in range(1, horizons):
        acc_a[...] += dot_nt(qg[k], wp_ref[k])

    def make_context_grad(rows):
        rounded = acc_a[rows, :].astype(BF16)
        cgv[1, rows, :] = rounded
        cgv[0, rows, :] = earlier(rounded.astype(F32), 1).astype(BF16)

    windows(make_context_grad)
    turned_latent = latent[...].T
    for half in range(2):
        share = dot(turned_latent, cgv[half]).astype(BF16).reshape(chips // 2, 2, prow, channels)
        for parity in range(2):
            stage[1, parity, half * (chips // 2) : (half + 1) * (chips // 2)] = share[:, parity]
    core_copy(1).start()
    core_done(0)
    acc_a[...] = dot_nt(cgv[1], wc_ref[1]) + dot_nt(cgv[0], wc_ref[0])

    each(n, lambda j: own_copy(j, dp_peer(j)).wait_recv())
    owned = lax.fori_loop(
        1, n, lambda j, total: total + own_in[dp_peer(j)].astype(F32), own_out[me].astype(F32)
    )
    high = owned.astype(BF16)
    low = (owned - high.astype(F32)).astype(BF16)
    acc_b[...] = jnp.zeros_like(acc_b)
    for k in range(horizons):
        mine = slice(k * per, (k + 1) * per)
        acc_b[...] += dot(chosen[k], high[mine]) + dot(chosen[k], low[mine])
    core_done(1)
    small_in[me] = jnp.zeros_like(small_in[me])

    def norm_back(rows):
        total = glat[rows, :] + acc_a[rows, :] + acc_b[rows, :]
        norm_row = normed[rows, :]
        small_in[me, 0:1] += jnp.sum(total * norm_row, axis=0, keepdims=True)
        grad = total * gain_ref[...]
        active_grad = inv[rows, :] * (
            grad
            - jnp.mean(grad, axis=1, keepdims=True)
            - norm_row * jnp.mean(grad * norm_row, axis=1, keepdims=True)
        )
        rounded = jnp.where(pre2[rows, :] > 0, active_grad, 0.0).astype(BF16)
        pv[1, rows, :] = rounded
        pv[0, rows, :] = earlier(rounded.astype(F32), 1).astype(BF16)

    windows(norm_back)

    blocks = channels // LANES
    seconds = pieces - 2

    def second(b, i):
        lhs = hid[lax.rem(b, quarters), :, i * LANES : (i + 1) * LANES]
        return dot_tn(lhs, pv[b // quarters]).astype(BF16)

    if prow == LANES:
        for i in range(seconds):

            def fill(parity, i=i):
                for h in range(quarters // 2):
                    turned = hid[2 * h + parity, :, i * LANES : (i + 1) * LANES].T
                    for v in range(2):
                        stage[2 + i, parity, h + v * (quarters // 2)] = dot(turned, pv[v]).astype(BF16)

            fill(1 - my_core)
            core_copy(2 + i).start()
            fill(my_core)
            if i > 0:
                core_done(1 + i)
            if i > 1:
                chip_done(i - 2)
    else:
        each_chips = LANES // (seconds * prow) // 2

        def fill(b, carry):
            for i in range(blocks):
                share = second(b, i).reshape(each_chips, 2, seconds, prow, channels)
                at = pl.ds((b * blocks + i) * each_chips, each_chips)
                for parity in range(2):
                    for s in range(seconds):
                        stage[2 + s, parity, at] = share[:, parity, s]
            return carry

        lax.fori_loop(0, 2 * quarters, fill, 0)
        for i in range(seconds):
            core_copy(2 + i).start()
            if i > 0:
                core_done(1 + i)
    core_done(pieces - 1)
    if prow != LANES:
        chip_done(0)
        chip_done(1)

    def first(q, carry):
        back = dot_nt(pv[1], w2_ref[q + quarters]) + dot_nt(pv[0], w2_ref[q])
        pre = dot(x_ref[...], w1[q])
        gfirst[q] = dot_tn(x_ref[...], jnp.where(pre > 0, back, 0.0).astype(BF16))
        return carry

    lax.fori_loop(0, quarters // 2, first, 0)
    z_done(0)
    z_done(1)
    chip_done(2)
    lax.fori_loop(quarters // 2, quarters, first, 0)
    chip_done(3)
    z_done(2)
    row = lax.broadcasted_iota(jnp.int32, (16, channels), 0)
    gain_row = small_in[me, 0:1]
    first_sum = gfirst[0, 0:16, :]
    for q in range(1, quarters):
        first_sum = first_sum + gfirst[q, taps // 2 * q : taps // 2 * q + 16, :]
    small_in[me] = (
        jnp.where(row < 10, first_sum, 0.0)
        + jnp.where(row == 10, gain_row, 0.0)
        + jnp.where(row == 11, loss_acc[...], 0.0)
    )

    def small_copy(j, slot):
        return to_dp(small_in.at[slot], small_in.at[slot], sdp_s.at[j], sdp_r.at[slot], dp_peer(j))

    def small_z_copy(j, slot):
        return to_z(small_z.at[slot], small_z.at[slot], sz_s.at[j], sz_r.at[slot], z_peer(j))

    each(n, lambda j: small_copy(j, me).start())
    for p in range(4, pieces):
        chip_done(p)
        z_done(p - 1)
    each(n, lambda j: small_copy(j, dp_peer(j)).wait_recv())
    small_z[zme] = lax.fori_loop(1, n, lambda j, total: total + small_in[j], small_in[0])
    each(g, lambda j: small_z_copy(j, zme).start())
    z_done(pieces - 1)
    each(g, lambda j: small_z_copy(j, z_peer(j)).wait_recv())
    small_ref[...] = lax.fori_loop(1, g, lambda j, total: total + small_z[j], small_z[0])
    for p in range(pieces):
        fin_done(p)

    def leave_dp(j):
        panel_copy(j, me).wait_send()
        own_copy(j, me).wait_send()
        small_copy(j, me).wait_send()

    each(n, leave_dp)
    each(g, lambda j: small_z_copy(j, zme).wait_send())
    for p in range(pieces):
        core_copy(p).wait_send()
        each(chips, lambda j, p=p: chip_copy(p, j, my_chip).wait_send())

        def leave_z(j, p=p):
            z_copy(p, j, zme).wait_send()
            fin_copy(p, j, zme).wait_send()

        each(g, leave_z)


def finish(count, fin_ref, small_ref, loss_ref, gf_ref, gs_ref, gg_ref, gc_ref, gp_ref):
    pieces, g, prow, cols = fin_ref.shape
    horizons, part, _ = gp_ref.shape
    for z in range(g):
        at = slice(z * cols, (z + 1) * cols)
        value = fin_ref[0, z].astype(F32)
        for k in range(horizons):
            gp_ref[k, :, at] = value[k * part : (k + 1) * part]
        gc_ref[:, at] = fin_ref[1, z].astype(F32)
        for p in range(2, pieces):
            gs_ref[(p - 2) * prow : (p - 1) * prow, at] = fin_ref[p, z].astype(F32)
    gf_ref[...] = small_ref[0:10, :]
    gg_ref[...] = small_ref[10:11, :]
    loss_ref[...] = small_ref[11:12, 0:1] / count


def frame_inputs(audio, starts):
    span = 20 * STEPS
    rows = []
    for w in range(starts.shape[0]):
        wave = lax.dynamic_slice(
            audio, (jnp.int32(0), starts[w]), (1, span), allow_negative_indices=False
        )
        steps = wave.reshape(STEPS, 20)
        before = jnp.concatenate([jnp.zeros((1, 5), wave.dtype), steps[:-1, 15:]], axis=0)
        rows.append(jnp.concatenate([before, steps], axis=1))
    return jnp.pad(jnp.concatenate(rows, axis=0), ((0, 0), (0, LANES - 25)))


def on_device(audio, starts, offsets, w_first, w_second, gain, w_context, w_predict):
    channels = w_second.shape[1]
    horizons = w_predict.shape[0]
    g = lax.axis_size("grp")
    n = lax.axis_size("dp")
    wins = starts.shape[0]
    tokens = wins * STEPS
    count = float(wins * g * n * (horizons * STEPS - horizons * (horizons + 1) // 2))
    x = frame_inputs(audio, starts)
    picks = offsets.shape[1] * offsets.shape[2]
    quarters = w_second.shape[0] // (2 * channels)
    prow = 2 * channels // n
    pieces = 2 + w_second.shape[0] // (2 * channels)
    chips = n // 2
    cols = channels // g
    panel_width = n * offsets.shape[2]
    vm = pltpu.VMEM
    dma = pltpu.SemaphoreType.DMA
    spec = pl.BlockSpec(memory_space=pltpu.VMEM)
    full = (tokens, channels)
    fin, small = pl.pallas_call(
        functools.partial(kernel, n, g, count),
        out_shape=(
            jax.ShapeDtypeStruct((pieces, g, prow, cols), BF16),
            jax.ShapeDtypeStruct((16, channels), F32),
        ),
        in_specs=[spec] * 7,
        out_specs=[spec] * 2,
        scratch_shapes=[
            vm((quarters, LANES, channels), BF16),
            vm((quarters,) + full, BF16),
            vm(full, F32),
            vm(full, F32),
            vm(full, F32),
            vm(full, F32),
            vm((tokens, 1), F32),
            vm(full, BF16),
            vm(full, BF16),
            vm((horizons,) + full, BF16),
            vm((tokens, panel_width), F32),
            vm((horizons, tokens, panel_width), BF16),
            vm((horizons,) + full, F32),
            vm((horizons,) + full, BF16),
            vm(full, F32),
            vm((2,) + full, BF16),
            vm((2,) + full, BF16),
            vm((quarters, LANES, channels), F32),
            vm((quarters, LANES, channels), F32),
            vm((n, picks, channels), BF16),
            vm((n, picks, channels), BF16),
            vm((n, picks, channels), BF16),
            vm((1, channels), F32),
            vm((n, 16, channels), F32),
            vm((g, 16, channels), F32),
            vm((pieces, 2, chips, prow, channels), BF16),
            vm((pieces, chips, prow, channels), BF16),
            vm((pieces, chips, prow, channels), BF16),
            vm((pieces, g, prow, cols), BF16),
            vm((pieces, g, prow, cols), BF16),
        ]
        + [dma((n,))] * 6
        + [dma((g,))] * 2
        + [dma((pieces,))] * 2
        + [dma((pieces, chips))] * 2
        + [dma((pieces, g))] * 4,
        compiler_params=pltpu.CompilerParams(
            collective_id=0, has_side_effects=True, vmem_limit_bytes=56 * 1024 * 1024
        ),
    )(
        offsets,
        x,
        w_first,
        w_second.reshape(2 * quarters, channels, channels),
        gain.reshape(1, channels),
        w_context.reshape(2, channels, channels),
        w_predict,
    )
    loss, gf, gs, gg, gc, gp = pl.pallas_call(
        functools.partial(finish, count),
        out_shape=(
            jax.ShapeDtypeStruct((1, 1), F32),
            jax.ShapeDtypeStruct(w_first.shape, F32),
            jax.ShapeDtypeStruct((w_second.shape[0] // n, channels), F32),
            jax.ShapeDtypeStruct((1, channels), F32),
            jax.ShapeDtypeStruct((w_context.shape[0] // n, channels), F32),
            jax.ShapeDtypeStruct((horizons, channels // n, channels), F32),
        ),
        in_specs=[spec] * 2,
        out_specs=[spec] * 6,
    )(fin, small)
    return (loss.reshape(()), gf, gs, gg.reshape(channels), gc, gp)


def solution(mesh):
    return jax.shard_map(
        on_device,
        mesh=mesh,
        in_specs=(
            P(("grp", "dp"), None),
            P(("grp", "dp")),
            P(("grp", "dp"), None, None),
            P(),
            P(),
            P(),
            P(),
            P(),
        ),
        out_specs=(P(), P(), P("dp", None), P(), P("dp", None), P(None, "dp", None)),
        check_vma=False,
    )
```
